512 devices in a mesh: var: 64 (over y, z_lo, core), ind: 8 (over x, z_hi).
Axes of the slice: x: 4, y: 4, z: 16 (z_hi: 2, z_lo: 8; z = z_hi * 8 + z_lo), core: 2. Of those that a mesh axis runs over, the one named last changes fastest.
Arguments:
- dosage: bfloat16 [16384, 32768], P('ind', 'var'), may hold values from 0 to 2
- positions: int32 [32768], replicated, may hold values from 10001 to 767829776, as said below
- partners: int32 [320], P('var'), may hold values from -1 to 63, as said below
Outputs:
- ld_tiles: bfloat16 [512, 320, 512], P('ind', 'var')
The draws below stay inside these ranges and needn't reach their ends.
Inputs may be any that keep to these rules, and one draw needn't show every extreme that they name: positions strictly increase along the segment. `partners`: slot s of block k holds k + s when block k + s exists and its first variant lies within 3000000 base pairs of block k's last variant, else -1; slot 0 always holds k, so the -1 slots come last.
All inputs are finite; a program needn't handle non-finite values.
Results may differ from the reference program's by a relative error of at most 0.015.
Values may be sent and summed in bfloat16 or wider, within the bound.
A program may use at most 64 MiB of HBM per device.

```python
import jax
import jax.numpy as jnp
from jax import lax

BLOCK = 512
WINDOW_BP = 3000000
IND_DEV = 2048
SLOTS = 5
IND = 16384
VARIANTS = 32768
N_VAR = 64
N_IND = 8


def window_tables(key):
    base_key = jax.random.fold_in(key, 5)
    level_key, gap_key = jax.random.split(base_key)
    block_total = VARIANTS // BLOCK
    regions = (block_total + 7) // 8
    density_level = jax.random.randint(level_key, (regions,), 0, 4)
    density_level = jnp.where(jnp.arange(regions) == 0, 0, density_level)
    per_variant = jnp.repeat(density_level, 8 * BLOCK)[:VARIANTS]
    gap_unit = WINDOW_BP // (2 * BLOCK)
    gap_limit = gap_unit * jnp.left_shift(jnp.ones_like(per_variant), per_variant)
    gap_sizes = jax.random.randint(gap_key, (VARIANTS,), 1, gap_limit + 1)
    gap_sizes = gap_sizes.at[0].set(1)
    earlier_total = jnp.sum(gap_sizes[:-1])
    gap_sizes = gap_sizes.at[VARIANTS - 1].set(8 * gap_unit * VARIANTS - earlier_total)
    locations = (10000 + jnp.cumsum(gap_sizes)).astype(jnp.int32)
    firsts = locations[::BLOCK]
    last_spots = locations[BLOCK - 1::BLOCK]
    block_ids = jnp.arange(block_total)
    slot_ids = jnp.arange(SLOTS)
    right_index = block_ids[:, None] + slot_ids[None, :]
    clipped = jnp.minimum(right_index, block_total - 1)
    within = (right_index < block_total) & (firsts[clipped] - last_spots[:, None] <= WINDOW_BP)
    partner_list = jnp.where(within, right_index, -1).astype(jnp.int32).reshape(-1)
    return (locations, partner_list)


def draw_positions(key, part):
    return window_tables(key)[0]


def draw_partners(key, part):
    return window_tables(key)[1]


def draw_dosage(key, part):
    key = jax.random.fold_in(key, 11)
    keys = jax.random.split(key, 7)
    block_total = VARIANTS // BLOCK
    lag_count = 5
    latent_width = (block_total + lag_count - 1) * BLOCK
    latent = jax.random.normal(keys[0], (IND, latent_width), jnp.float32)
    own_noise = jax.random.normal(keys[1], (IND, VARIANTS), jnp.float32)
    order_keys = jax.random.split(keys[6], block_total * lag_count)
    orders = jax.vmap(lambda single_key: jax.random.permutation(single_key, BLOCK))(order_keys)
    orders = orders.reshape(block_total, lag_count, BLOCK)
    block_ids = jnp.arange(block_total)
    shared = jnp.zeros((IND, VARIANTS), jnp.float32)
    for back in range(lag_count):
        source = ((block_ids + lag_count - 1 - back)[:, None] * BLOCK + orders[:, back, :]).reshape(-1)
        shared = shared + jnp.take(latent, source, axis=1)
    shared = shared / lag_count ** 0.5
    loading = jax.random.uniform(keys[2], (VARIANTS,), jnp.float32, 0.7, 1.3)
    loading = loading * jnp.where(jax.random.uniform(keys[3], (VARIANTS,)) < 0.5, -1.0, 1.0)
    offset_logit = jax.random.uniform(keys[4], (VARIANTS,), jnp.float32, -1.0, 1.0)
    ancestry_slope = jax.random.uniform(keys[5], (VARIANTS,), jnp.float32, 0.3, 0.7)
    ancestry = -1.2 + 2.4 * jnp.arange(IND, dtype=jnp.float32) / (IND - 1)
    logit_value = offset_logit[None, :] + ancestry[:, None] * ancestry_slope[None, :]
    logit_value = logit_value + 1.2 * loading[None, :] * shared + 0.5 * own_noise
    return (2.0 * jax.nn.sigmoid(logit_value)).astype(jnp.bfloat16)


def setup_inputs(seed: int = 0) -> dict:
    key_list = jax.random.split(jax.random.key(seed), 4)
    return {
        "dosage": draw_dosage(jax.random.fold_in(key_list[3], 71), 0),
        "positions": draw_positions(jax.random.fold_in(key_list[3], 71), 0),
        "partners": draw_partners(jax.random.fold_in(key_list[3], 71), 0),
    }


def reference(dosage, positions, partners):
    values = dosage.astype(jnp.float32)
    first_sum = lax.optimization_barrier(jnp.sum(values, axis=0))
    second_sum = lax.optimization_barrier(jnp.sum(values * values, axis=0))
    average = first_sum / IND
    spread = second_sum / IND - average * average
    inverse = lax.rsqrt(spread + 1e-06)
    slot_table = partners.reshape(N_VAR, SLOTS)

    def scaled_block(block_number):
        block_number = jnp.minimum(block_number, N_VAR - 1).astype(jnp.int32)
        start_index = (block_number * BLOCK).astype(jnp.int32)
        raw_part = lax.dynamic_slice_in_dim(dosage, start_index, BLOCK, 1).astype(jnp.float32)
        mean_part = lax.dynamic_slice_in_dim(average, start_index, BLOCK)
        scale_part = lax.dynamic_slice_in_dim(inverse, start_index, BLOCK)
        spots = lax.dynamic_slice_in_dim(positions, start_index, BLOCK)
        return (((raw_part - mean_part) * scale_part).astype(jnp.bfloat16), spots)

    def one_block(block_index):
        own_block, own_spots = scaled_block(block_index)
        right_parts = [scaled_block(block_index + offset) for offset in range(SLOTS)]
        right_data = jnp.stack([part[0] for part in right_parts], axis=1)
        right_spots = jnp.stack([part[1] for part in right_parts], axis=0)
        left_block = own_block.astype(jnp.float32).reshape(N_IND, IND_DEV, BLOCK)
        right_block = right_data.astype(jnp.float32).reshape(N_IND, IND_DEV, SLOTS, BLOCK)
        partial_value = jnp.einsum('inc,inpb->icpb', left_block, right_block, precision=lax.Precision.HIGHEST)
        rounded = lax.optimization_barrier(partial_value.astype(jnp.bfloat16)).astype(jnp.float32)
        correlation = lax.optimization_barrier(jnp.sum(rounded, axis=0)) / IND
        inside = jnp.abs(right_spots[None, :, :] - own_spots[:, None, None]) <= WINDOW_BP
        kept_mask = inside & (slot_table[block_index] >= 0)[None, :, None]
        return jnp.where(kept_mask, correlation, jnp.float32(0.0)).astype(jnp.bfloat16)
    blocks = lax.map(one_block, jnp.arange(N_VAR, dtype=jnp.int32))
    return blocks.transpose(1, 0, 2, 3).reshape(BLOCK, N_VAR * SLOTS, BLOCK)
```

```python
import jax
import jax.numpy as jnp
from jax import lax
from jax.experimental import pallas as pl
from jax.experimental.pallas import tpu as pltpu
from jax.sharding import PartitionSpec as P

WINDOW_BP = 3000000
MESH = pl.DeviceIdType.MESH

CHUNKS = 4
WIDE = 128
SLAB = 256


def kernel(
    dosage, out, raw, stats, left, pair, partial, from_x, to_z, kept, from_z, mom, mom_x, mom_z,
    load_sem, d_send, d_recv, r_send, r_recv, t_send, t_recv, u_send, u_recv,
    m_send, m_recv, x_send, x_recv, z_send, z_recv,
):
    v, i = lax.axis_index("var"), lax.axis_index("ind")
    rows = dosage.shape[0]
    blocks = lax.axis_size("var")
    people = rows * lax.axis_size("ind")
    core = lax.rem(v, 2)
    x, zh = lax.div(i, 2), lax.rem(i, 2)
    below = (jnp.maximum(v - 2, 0), i)
    above = (jnp.minimum(v + 2, blocks - 1), i)
    sibling = (v + 1 - 2 * core, i)
    opposite = (v, i + 1 - 2 * zh)

    def x_peer(d):
        return lax.rem(x + d, 4)

    has_below, has_above, has_above2 = v >= 2, v + 2 < blocks, lax.div(v, 2) + 2 < lax.div(blocks, 2)

    barrier = pltpu.get_barrier_semaphore()
    for d in (1, 2, 3):
        pl.semaphore_signal(barrier, inc=1, device_id=(v, 2 * x_peer(d) + zh), device_id_type=MESH)
    pl.semaphore_signal(barrier, inc=1, device_id=sibling, device_id_type=MESH)
    pl.semaphore_signal(barrier, inc=1, device_id=opposite, device_id_type=MESH)

    @pl.when(has_below)
    def _():
        pl.semaphore_signal(barrier, inc=1, device_id=below, device_id_type=MESH)

    @pl.when(has_above)
    def _():
        pl.semaphore_signal(barrier, inc=1, device_id=above, device_id_type=MESH)

    def load(j):
        return pltpu.make_async_copy(dosage.at[:, pl.ds(j * WIDE, WIDE)], raw.at[0, j], load_sem.at[j])

    for j in range(CHUNKS):
        load(j).start()

    greeted = 5 + jnp.minimum(lax.div(v, 2), 1) + jnp.minimum(lax.div(blocks - 1 - v, 2), 1)
    pl.semaphore_wait(barrier, greeted)

    def remote(src, dst, send, recv, to):
        return pltpu.make_async_remote_copy(
            src_ref=src, dst_ref=dst, send_sem=send, recv_sem=recv, device_id=to, device_id_type=MESH
        )

    def send_own(j):
        return remote(raw.at[0, j], raw.at[2, j], d_send.at[0, j], d_recv.at[0, j], below)

    def forward(j):
        return remote(raw.at[2, j], raw.at[4, j], d_send.at[1, j], d_recv.at[1, j], below)

    def second(phase):
        return 3 - 2 * core if phase == 0 else 1 + 2 * core

    def passed(phase):
        return 2 if phase == 0 else 4 - 4 * core

    def sibling_second(phase):
        return 1 + 2 * core if phase == 0 else 3 - 2 * core

    def relay(phase, j):
        return remote(
            raw.at[passed(phase), j], raw.at[sibling_second(phase), j], r_send.at[phase, j], r_recv.at[phase, j], sibling
        )

    def relay_arrival(phase, j):
        return remote(raw.at[0, j], raw.at[second(phase), j], r_send.at[phase, j], r_recv.at[phase, j], sibling)

    def stats_send(phase):
        return remote(stats.at[2 * phase], stats.at[2 + 2 * phase], t_send.at[phase], t_recv.at[phase], below)

    def stats_relay(phase):
        return remote(
            stats.at[passed(phase)], stats.at[sibling_second(phase)], u_send.at[phase], u_recv.at[phase], sibling
        )

    def stats_relay_arrival(phase):
        return remote(stats.at[0], stats.at[second(phase)], u_send.at[phase], u_recv.at[phase], sibling)

    arrives = [has_above, has_above2]
    relays = [has_above, (core == 1) | has_above2]
    relayed = [has_above, (core == 0) | has_above2]

    for j in range(CHUNKS):
        load(j).wait()

        @pl.when(has_below)
        def _():
            send_own(j).start()

    for j in range(CHUNKS):

        def add_up(n, totals):
            part = raw[0, j, pl.ds(pl.multiple_of(n * SLAB, SLAB), SLAB), :].astype(jnp.float32)
            return totals[0] + jnp.sum(part, axis=0, keepdims=True), totals[1] + jnp.sum(
                part * part, axis=0, keepdims=True
            )

        zero = jnp.zeros((1, WIDE), jnp.float32)
        first, squares = lax.fori_loop(0, rows // SLAB, add_up, (zero, zero))
        mom[j, 0:1, :] = first
        mom[j, 1:2, :] = squares
        mom[j, 2:8, :] = jnp.zeros((6, WIDE), jnp.float32)

    def moments_x(d):
        return remote(mom, mom_x.at[d - 1], m_send.at[d - 1], m_recv.at[d - 1], (v, 2 * x_peer(d) + zh))

    for d in (2, 1, 3):
        moments_x(d).start()
    for d in (1, 2, 3):
        moments_x(d).wait_recv()
    mom_z[0] = (mom[...] + mom_x[1]) + (mom_x[0] + mom_x[2])
    moments_z = remote(mom_z.at[0], mom_z.at[1], m_send.at[3], m_recv.at[3], opposite)
    moments_z.start()
    moments_z.wait_recv()
    total = mom_z[0] + mom_z[1]
    average = total[:, 0:1, :] / people
    spread = total[:, 1:2, :] / people - average * average
    stats[0, :, 0:1, :] = average
    stats[0, :, 1:2, :] = lax.rsqrt(spread + 1e-06)
    stats[0, :, 2:8, :] = jnp.zeros((CHUNKS, 6, WIDE), jnp.float32)

    @pl.when(has_below)
    def _():
        stats_send(0).start()

    def scale(slot, j, column):
        average = stats[slot, j, 0:1, :]
        inverse = stats[slot, j, 1:2, :]

        def body(n, carry):
            where = pl.ds(pl.multiple_of(n * SLAB, SLAB), SLAB)
            values = raw[slot, j, where, :].astype(jnp.float32)
            pair[where, pl.ds(column * WIDE, WIDE)] = ((values - average) * inverse).astype(jnp.bfloat16)
            return carry

        lax.fori_loop(0, rows // SLAB, body, 0)

    def turn(column, j):
        def body(n, carry):
            where = pl.ds(pl.multiple_of(n * SLAB, SLAB), SLAB)
            part = pair[where, pl.ds(column * WIDE, WIDE)]
            left[pl.ds(j * WIDE, WIDE), where] = part.T
            return carry

        lax.fori_loop(0, rows // SLAB, body, 0)

    def share_x(t, d):
        to = x_peer(d)
        return remote(
            partial.at[t, pl.ds(pl.multiple_of(to * 128, 128), 128)], from_x.at[t, d - 1],
            x_send.at[t, d - 1], x_recv.at[t, d - 1], (v, 2 * to + zh),
        )

    def share_z(t):
        return remote(to_z.at[t], from_z.at[t], z_send.at[t], z_recv.at[t], opposite)

    def multiply(t):
        partial[t] = jnp.dot(left[...], pair[...], preferred_element_type=jnp.float32).astype(jnp.bfloat16)
        for d in (2, 1, 3):
            share_x(t, d).start()

    def half(t, which):
        own = pl.ds(pl.multiple_of(x * 128 + which * 64, 64), 64)
        there = pl.ds(pl.multiple_of(which * 64, 64), 64)
        return (partial[t, own, :].astype(jnp.float32) + from_x[t, 1, there, :].astype(jnp.float32)) + (
            from_x[t, 0, there, :].astype(jnp.float32) + from_x[t, 2, there, :].astype(jnp.float32)
        )

    def reduce(t):
        for d in (1, 2, 3):
            share_x(t, d).wait_recv()
        to_z[t] = half(t, 1 - zh).astype(jnp.bfloat16)
        share_z(t).start()
        kept[t] = half(t, zh)

    def finish(t, first_slot, first_chunk, second_slot, second_chunk):
        share_z(t).wait_recv()
        total = (kept[t] + from_z[t].astype(jnp.float32)) / people
        out[first_slot, first_chunk] = total[:, :WIDE]
        out[second_slot, second_chunk] = total[:, WIDE:]

    for t in (1, 0):
        for column in range(2):
            scale(0, 2 * t + column, column)
            turn(column, 2 * t + column)
    multiply(0)
    for column in range(2):
        scale(0, 2 + column, column)
    multiply(1)
    for t in range(2):
        reduce(t)

    for phase in range(2):

        @pl.when(arrives[phase])
        def _():
            stats_send(phase).wait_recv()

        if phase == 0:

            @pl.when(has_below & has_above)
            def _():
                stats_send(1).start()

        @pl.when(relays[phase])
        def _():
            stats_relay(phase).start()

        @pl.when(relayed[phase])
        def _():
            stats_relay_arrival(phase).wait_recv()

        def step(j, carry):
            @pl.when(arrives[phase])
            def _():
                (send_own if phase == 0 else forward)(j).wait_recv()

            if phase == 0:

                @pl.when(has_below & has_above)
                def _():
                    forward(j).start()

            @pl.when(relays[phase])
            def _():
                relay(phase, j).start()

            scale(2 + 2 * phase, j, 0)

            @pl.when(relayed[phase])
            def _():
                relay_arrival(phase, j).wait_recv()

            scale(second(phase), j, 1)
            t = 2 + 4 * phase + j
            multiply(t)
            reduce(t)
            return carry

        lax.fori_loop(0, CHUNKS, step, 0)

    for t in range(2):
        finish(t, 0, 2 * t, 0, 2 * t + 1)
    for phase in range(2):

        def last(j, carry):
            finish(2 + 4 * phase + j, 2 + 2 * phase, j, second(phase), j)
            return carry

        lax.fori_loop(0, CHUNKS, last, 0)

    for d in (1, 2, 3):
        moments_x(d).wait_send()
    moments_z.wait_send()

    @pl.when(has_below)
    def _():
        stats_send(0).wait_send()

    @pl.when(has_below & has_above)
    def _():
        stats_send(1).wait_send()

    for phase in range(2):

        @pl.when(relays[phase])
        def _():
            stats_relay(phase).wait_send()

    def drain(j, carry):
        @pl.when(has_below)
        def _():
            send_own(j).wait_send()

        @pl.when(has_below & has_above)
        def _():
            forward(j).wait_send()

        for phase in range(2):

            @pl.when(relays[phase])
            def _():
                relay(phase, j).wait_send()

        return carry

    lax.fori_loop(0, CHUNKS, drain, 0)

    def drain_sums(t, carry):
        for d in (1, 2, 3):
            share_x(t, d).wait_send()
        share_z(t).wait_send()
        return carry

    lax.fori_loop(0, 2 + 2 * CHUNKS, drain_sums, 0)


def sums(dosage):
    rows, width = dosage.shape
    steps = 2 + 2 * CHUNKS
    dma = pltpu.SemaphoreType.DMA
    return pl.pallas_call(
        kernel,
        out_shape=jax.ShapeDtypeStruct((5, CHUNKS, 64, WIDE), jnp.float32),
        in_specs=[pl.BlockSpec(memory_space=pl.ANY)],
        out_specs=pl.BlockSpec(memory_space=pltpu.VMEM),
        scratch_shapes=[
            pltpu.VMEM((5, CHUNKS, rows, WIDE), jnp.bfloat16),
            pltpu.VMEM((5, CHUNKS, 8, WIDE), jnp.float32),
            pltpu.VMEM((width, rows), jnp.bfloat16),
            pltpu.VMEM((rows, 2 * WIDE), jnp.bfloat16),
            pltpu.VMEM((steps, width, 2 * WIDE), jnp.bfloat16),
            pltpu.VMEM((steps, 3, 128, 2 * WIDE), jnp.bfloat16),
            pltpu.VMEM((steps, 64, 2 * WIDE), jnp.bfloat16),
            pltpu.VMEM((steps, 64, 2 * WIDE), jnp.float32),
            pltpu.VMEM((steps, 64, 2 * WIDE), jnp.bfloat16),
            pltpu.VMEM((CHUNKS, 8, WIDE), jnp.float32),
            pltpu.VMEM((3, CHUNKS, 8, WIDE), jnp.float32),
            pltpu.VMEM((2, CHUNKS, 8, WIDE), jnp.float32),
            dma((CHUNKS,)),
            dma((2, CHUNKS)), dma((2, CHUNKS)), dma((2, CHUNKS)), dma((2, CHUNKS)),
            dma((2,)), dma((2,)), dma((2,)), dma((2,)),
            dma((4,)), dma((4,)),
            dma((steps, 3)), dma((steps, 3)), dma((steps,)), dma((steps,)),
        ],
        compiler_params=pltpu.CompilerParams(
            collective_id=0, has_side_effects=True, vmem_limit_bytes=48 * 2**20
        ),
    )(dosage)


def per_device(dosage, positions, partners):
    block_width = dosage.shape[1]
    group_count = lax.axis_size("ind")
    var_index = lax.axis_index("var")
    group_index = lax.axis_index("ind")
    slot_count = partners.shape[0]
    usable = partners >= 0
    share_rows = block_width // group_count
    correlation = sums(dosage).transpose(2, 0, 1, 3).reshape(share_rows, slot_count, block_width)
    block_total = positions.shape[0] // block_width
    left_spots = lax.dynamic_slice_in_dim(
        positions, var_index * block_width + group_index * share_rows, share_rows
    )
    right_spots = jnp.stack(
        [
            lax.dynamic_slice_in_dim(
                positions,
                jnp.minimum(var_index + offset, block_total - 1) * block_width,
                block_width,
            )
            for offset in range(slot_count)
        ],
        axis=0,
    )
    inside = jnp.abs(right_spots[None, :, :] - left_spots[:, None, None]) <= WINDOW_BP
    kept_mask = inside & usable[None, :, None]
    return jnp.where(kept_mask, correlation, jnp.float32(0.0)).astype(jnp.bfloat16)


def solution(mesh):
    return jax.shard_map(
        per_device,
        mesh=mesh,
        in_specs=(P("ind", "var"), P(), P("var")),
        out_specs=P("ind", "var", None),
        check_vma=False,
    )
```

```python
import jax
import jax.numpy as jnp
from jax import lax
from jax.experimental import pallas as pl
from jax.experimental.pallas import tpu as pltpu
from jax.sharding import PartitionSpec as P

WINDOW_BP = 3000000
MESH = pl.DeviceIdType.MESH

CHUNKS = 4
WIDE = 128
SLAB = 256


def kernel(
    dosage, positions, partners, out, raw, stats, left, pair, partial, from_x, to_z, kept, from_z, mom, mom_x, mom_z, spots,
    load_sem, d_send, d_recv, r_send, r_recv, t_send, t_recv, u_send, u_recv,
    m_send, m_recv, x_send, x_recv, z_send, z_recv,
):
    v, i = lax.axis_index("var"), lax.axis_index("ind")
    rows = dosage.shape[0]
    blocks = lax.axis_size("var")
    people = rows * lax.axis_size("ind")
    core = lax.rem(v, 2)
    x, zh = lax.div(i, 2), lax.rem(i, 2)
    below = (jnp.maximum(v - 2, 0), i)
    above = (jnp.minimum(v + 2, blocks - 1), i)
    sibling = (v + 1 - 2 * core, i)
    opposite = (v, i + 1 - 2 * zh)

    def x_peer(d):
        return lax.rem(x + d, 4)

    has_below, has_above, has_above2 = v >= 2, v + 2 < blocks, lax.div(v, 2) + 2 < lax.div(blocks, 2)

    barrier = pltpu.get_barrier_semaphore()
    for d in (1, 2, 3):
        pl.semaphore_signal(barrier, inc=1, device_id=(v, 2 * x_peer(d) + zh), device_id_type=MESH)
    pl.semaphore_signal(barrier, inc=1, device_id=sibling, device_id_type=MESH)
    pl.semaphore_signal(barrier, inc=1, device_id=opposite, device_id_type=MESH)

    @pl.when(has_below)
    def _():
        pl.semaphore_signal(barrier, inc=1, device_id=below, device_id_type=MESH)

    @pl.when(has_above)
    def _():
        pl.semaphore_signal(barrier, inc=1, device_id=above, device_id_type=MESH)

    def load(j):
        return pltpu.make_async_copy(dosage.at[:, pl.ds(j * WIDE, WIDE)], raw.at[0, j], load_sem.at[j])

    for j in range(CHUNKS):
        load(j).start()

    greeted = 5 + jnp.minimum(lax.div(v, 2), 1) + jnp.minimum(lax.div(blocks - 1 - v, 2), 1)
    pl.semaphore_wait(barrier, greeted)

    def remote(src, dst, send, recv, to):
        return pltpu.make_async_remote_copy(
            src_ref=src, dst_ref=dst, send_sem=send, recv_sem=recv, device_id=to, device_id_type=MESH
        )

    def send_own(j):
        return remote(raw.at[0, j], raw.at[2, j], d_send.at[0, j], d_recv.at[0, j], below)

    def forward(j):
        return remote(raw.at[2, j], raw.at[4, j], d_send.at[1, j], d_recv.at[1, j], below)

    def second(phase):
        return 3 - 2 * core if phase == 0 else 1 + 2 * core

    def passed(phase):
        return 2 if phase == 0 else 4 - 4 * core

    def sibling_second(phase):
        return 1 + 2 * core if phase == 0 else 3 - 2 * core

    def relay(phase, j):
        return remote(
            raw.at[passed(phase), j], raw.at[sibling_second(phase), j], r_send.at[phase, j], r_recv.at[phase, j], sibling
        )

    def relay_arrival(phase, j):
        return remote(raw.at[0, j], raw.at[second(phase), j], r_send.at[phase, j], r_recv.at[phase, j], sibling)

    def stats_send(phase):
        return remote(stats.at[2 * phase], stats.at[2 + 2 * phase], t_send.at[phase], t_recv.at[phase], below)

    def stats_relay(phase):
        return remote(
            stats.at[passed(phase)], stats.at[sibling_second(phase)], u_send.at[phase], u_recv.at[phase], sibling
        )

    def stats_relay_arrival(phase):
        return remote(stats.at[0], stats.at[second(phase)], u_send.at[phase], u_recv.at[phase], sibling)

    arrives = [has_above, has_above2]
    relays = [has_above, (core == 1) | has_above2]
    relayed = [has_above, (core == 0) | has_above2]

    for j in range(CHUNKS):
        load(j).wait()
        if j < CHUNKS // 2:

            @pl.when(has_below)
            def _():
                send_own(j).start()

    for j in range(CHUNKS):

        def add_up(n, totals):
            part = raw[0, j, pl.ds(pl.multiple_of(n * SLAB, SLAB), SLAB), :].astype(jnp.float32)
            return totals[0] + jnp.sum(part, axis=0, keepdims=True), totals[1] + jnp.sum(
                part * part, axis=0, keepdims=True
            )

        zero = jnp.zeros((1, WIDE), jnp.float32)
        first, squares = lax.fori_loop(0, rows // SLAB, add_up, (zero, zero))
        mom[j, 0:1, :] = first
        mom[j, 1:2, :] = squares
        mom[j, 2:8, :] = jnp.zeros((6, WIDE), jnp.float32)

    def moments_x(d):
        return remote(mom, mom_x.at[d - 1], m_send.at[d - 1], m_recv.at[d - 1], (v, 2 * x_peer(d) + zh))

    for d in (2, 1, 3):
        moments_x(d).start()
    for d in (1, 2, 3):
        moments_x(d).wait_recv()
    mom_z[0] = (mom[...] + mom_x[1]) + (mom_x[0] + mom_x[2])
    moments_z = remote(mom_z.at[0], mom_z.at[1], m_send.at[3], m_recv.at[3], opposite)
    moments_z.start()
    moments_z.wait_recv()
    total = mom_z[0] + mom_z[1]
    average = total[:, 0:1, :] / people
    spread = total[:, 1:2, :] / people - average * average
    stats[0, :, 0:1, :] = average
    stats[0, :, 1:2, :] = lax.rsqrt(spread + 1e-06)
    stats[0, :, 2:8, :] = jnp.zeros((CHUNKS, 6, WIDE), jnp.float32)

    @pl.when(has_below)
    def _():
        stats_send(0).start()
        for j in range(CHUNKS // 2, CHUNKS):
            send_own(j).start()

    line = positions[pl.ds(4 * v + x, 1), :]
    spots[...] = jnp.broadcast_to(line, (128, 128)).T

    def scale(slot, j, column):
        average = stats[slot, j, 0:1, :]
        inverse = stats[slot, j, 1:2, :]

        def body(n, carry):
            where = pl.ds(pl.multiple_of(n * SLAB, SLAB), SLAB)
            values = raw[slot, j, where, :].astype(jnp.float32)
            pair[where, pl.ds(column * WIDE, WIDE)] = ((values - average) * inverse).astype(jnp.bfloat16)
            return carry

        lax.fori_loop(0, rows // SLAB, body, 0)

    def turn(column, j):
        def body(n, carry):
            where = pl.ds(pl.multiple_of(n * SLAB, SLAB), SLAB)
            part = pair[where, pl.ds(column * WIDE, WIDE)]
            left[pl.ds(j * WIDE, WIDE), where] = part.T
            return carry

        lax.fori_loop(0, rows // SLAB, body, 0)

    def share_x(t, d):
        to = x_peer(d)
        return remote(
            partial.at[t, pl.ds(pl.multiple_of(to * 128, 128), 128)], from_x.at[t, d - 1],
            x_send.at[t, d - 1], x_recv.at[t, d - 1], (v, 2 * to + zh),
        )

    def share_z(t):
        return remote(to_z.at[t], from_z.at[t], z_send.at[t], z_recv.at[t], opposite)

    def multiply(t):
        partial[t] = jnp.dot(left[...], pair[...], preferred_element_type=jnp.float32).astype(jnp.bfloat16)
        for d in (2, 1, 3):
            share_x(t, d).start()

    def half(t, which):
        own = pl.ds(pl.multiple_of(x * 128 + which * 64, 64), 64)
        there = pl.ds(pl.multiple_of(which * 64, 64), 64)
        return (partial[t, own, :].astype(jnp.float32) + from_x[t, 1, there, :].astype(jnp.float32)) + (
            from_x[t, 0, there, :].astype(jnp.float32) + from_x[t, 2, there, :].astype(jnp.float32)
        )

    def reduce(t):
        for d in (1, 2, 3):
            share_x(t, d).wait_recv()
        to_z[t] = half(t, 1 - zh).astype(jnp.bfloat16)
        share_z(t).start()
        kept[t] = half(t, zh)

    def finish(t, first_slot, first_chunk, second_slot, second_chunk):
        share_z(t).wait_recv()
        total = (kept[t] + from_z[t].astype(jnp.float32)) / people
        own_spots = spots[pl.ds(pl.multiple_of(zh * 64, 64), 64), :]
        for column, slot, chunk in ((0, first_slot, first_chunk), (1, second_slot, second_chunk)):
            place = jnp.minimum(v + slot, blocks - 1) * CHUNKS + chunk
            inside = jnp.abs(positions[pl.ds(place, 1), :] - own_spots) <= WINDOW_BP
            usable = jnp.where(inside, partners[slot], -1) >= 0
            out[slot, chunk] = jnp.where(usable, total[:, column * WIDE : (column + 1) * WIDE], 0.0)

    for t in (1, 0):
        for column in range(2):
            scale(0, 2 * t + column, column)
            turn(column, 2 * t + column)
    multiply(0)
    for column in range(2):
        scale(0, 2 + column, column)
    multiply(1)
    reduce(0)

    for phase in range(2):

        @pl.when(arrives[phase])
        def _():
            stats_send(phase).wait_recv()

        if phase == 0:

            @pl.when(has_below & has_above)
            def _():
                stats_send(1).start()

        @pl.when(relays[phase])
        def _():
            stats_relay(phase).start()

        @pl.when(relayed[phase])
        def _():
            stats_relay_arrival(phase).wait_recv()

        def step(j, carry):
            @pl.when(arrives[phase])
            def _():
                (send_own if phase == 0 else forward)(j).wait_recv()

            if phase == 0:

                @pl.when(has_below & has_above)
                def _():
                    forward(j).start()

            @pl.when(relays[phase])
            def _():
                relay(phase, j).start()

            scale(2 + 2 * phase, j, 0)

            @pl.when(relayed[phase])
            def _():
                relay_arrival(phase, j).wait_recv()

            scale(second(phase), j, 1)
            t = 2 + 4 * phase + j
            multiply(t)
            reduce(t - 1)
            return carry

        lax.fori_loop(0, CHUNKS, step, 0)

    for t in range(2):
        finish(t, 0, 2 * t, 0, 2 * t + 1)
    reduce(1 + 2 * CHUNKS)
    for phase in range(2):

        def last(j, carry):
            finish(2 + 4 * phase + j, 2 + 2 * phase, j, second(phase), j)
            return carry

        lax.fori_loop(0, CHUNKS, last, 0)

    for d in (1, 2, 3):
        moments_x(d).wait_send()
    moments_z.wait_send()

    @pl.when(has_below)
    def _():
        stats_send(0).wait_send()

    @pl.when(has_below & has_above)
    def _():
        stats_send(1).wait_send()

    for phase in range(2):

        @pl.when(relays[phase])
        def _():
            stats_relay(phase).wait_send()

    def drain(j, carry):
        @pl.when(has_below)
        def _():
            send_own(j).wait_send()

        @pl.when(has_below & has_above)
        def _():
            forward(j).wait_send()

        for phase in range(2):

            @pl.when(relays[phase])
            def _():
                relay(phase, j).wait_send()

        return carry

    lax.fori_loop(0, CHUNKS, drain, 0)

    def drain_sums(t, carry):
        for d in (1, 2, 3):
            share_x(t, d).wait_send()
        share_z(t).wait_send()
        return carry

    lax.fori_loop(0, 2 + 2 * CHUNKS, drain_sums, 0)


def tiles(dosage, positions, partners):
    rows, width = dosage.shape
    steps = 2 + 2 * CHUNKS
    dma = pltpu.SemaphoreType.DMA
    return pl.pallas_call(
        kernel,
        out_shape=jax.ShapeDtypeStruct((5, CHUNKS, 64, WIDE), jnp.float32),
        in_specs=[
            pl.BlockSpec(memory_space=pl.ANY),
            pl.BlockSpec(memory_space=pltpu.VMEM),
            pl.BlockSpec(memory_space=pltpu.SMEM),
        ],
        out_specs=pl.BlockSpec(memory_space=pltpu.VMEM),
        scratch_shapes=[
            pltpu.VMEM((5, CHUNKS, rows, WIDE), jnp.bfloat16),
            pltpu.VMEM((5, CHUNKS, 8, WIDE), jnp.float32),
            pltpu.VMEM((width, rows), jnp.bfloat16),
            pltpu.VMEM((rows, 2 * WIDE), jnp.bfloat16),
            pltpu.VMEM((steps, width, 2 * WIDE), jnp.bfloat16),
            pltpu.VMEM((steps, 3, 128, 2 * WIDE), jnp.bfloat16),
            pltpu.VMEM((steps, 64, 2 * WIDE), jnp.bfloat16),
            pltpu.VMEM((steps, 64, 2 * WIDE), jnp.float32),
            pltpu.VMEM((steps, 64, 2 * WIDE), jnp.bfloat16),
            pltpu.VMEM((CHUNKS, 8, WIDE), jnp.float32),
            pltpu.VMEM((3, CHUNKS, 8, WIDE), jnp.float32),
            pltpu.VMEM((2, CHUNKS, 8, WIDE), jnp.float32),
            pltpu.VMEM((128, 128), jnp.int32),
            dma((CHUNKS,)),
            dma((2, CHUNKS)), dma((2, CHUNKS)), dma((2, CHUNKS)), dma((2, CHUNKS)),
            dma((2,)), dma((2,)), dma((2,)), dma((2,)),
            dma((4,)), dma((4,)),
            dma((steps, 3)), dma((steps, 3)), dma((steps,)), dma((steps,)),
        ],
        compiler_params=pltpu.CompilerParams(
            collective_id=0, has_side_effects=True, vmem_limit_bytes=60 * 2**20
        ),
    )(dosage, positions.reshape(-1, WIDE), partners)


def per_device(dosage, positions, partners):
    masked = tiles(dosage, positions, partners)
    share_rows = masked.shape[2]
    return masked.transpose(2, 0, 1, 3).reshape(share_rows, partners.shape[0], dosage.shape[1]).astype(jnp.bfloat16)


def solution(mesh):
    return jax.shard_map(
        per_device,
        mesh=mesh,
        in_specs=(P("ind", "var"), P(), P("var")),
        out_specs=P("ind", "var", None),
        check_vma=False,
    )
```

```python
import jax
import jax.numpy as jnp
from jax import lax
from jax.experimental import pallas as pl
from jax.experimental.pallas import tpu as pltpu
from jax.sharding import PartitionSpec as P

WINDOW_BP = 3000000
MESH = pl.DeviceIdType.MESH

CHUNKS = 4
WIDE = 128
SLAB = 256


def kernel(
    dosage, positions, partners, out, raw, stats, left, pair, partial, from_x, to_z, kept, from_z, mom, mom_x, mom_z, spots, along, down,
    load_sem, d_send, d_recv, r_send, r_recv, t_send, t_recv, u_send, u_recv,
    m_send, m_recv, x_send, x_recv, z_send, z_recv,
):
    v, i = lax.axis_index("var"), lax.axis_index("ind")
    rows = dosage.shape[0]
    blocks = lax.axis_size("var")
    people = rows * lax.axis_size("ind")
    core = lax.rem(v, 2)
    x, zh = lax.div(i, 2), lax.rem(i, 2)
    below = (jnp.maximum(v - 2, 0), i)
    above = (jnp.minimum(v + 2, blocks - 1), i)
    sibling = (v + 1 - 2 * core, i)
    opposite = (v, i + 1 - 2 * zh)

    def x_peer(d):
        return lax.rem(x + d, 4)

    has_below, has_above, has_above2 = v >= 2, v + 2 < blocks, lax.div(v, 2) + 2 < lax.div(blocks, 2)

    barrier = pltpu.get_barrier_semaphore()
    for d in (1, 2, 3):
        pl.semaphore_signal(barrier, inc=1, device_id=(v, 2 * x_peer(d) + zh), device_id_type=MESH)
    pl.semaphore_signal(barrier, inc=1, device_id=sibling, device_id_type=MESH)
    pl.semaphore_signal(barrier, inc=1, device_id=opposite, device_id_type=MESH)

    @pl.when(has_below)
    def _():
        pl.semaphore_signal(barrier, inc=1, device_id=below, device_id_type=MESH)

    @pl.when(has_above)
    def _():
        pl.semaphore_signal(barrier, inc=1, device_id=above, device_id_type=MESH)

    def load(j):
        return pltpu.make_async_copy(dosage.at[:, pl.ds(j * WIDE, WIDE)], raw.at[0, j], load_sem.at[j])

    for j in range(CHUNKS):
        load(j).start()

    greeted = 5 + jnp.minimum(lax.div(v, 2), 1) + jnp.minimum(lax.div(blocks - 1 - v, 2), 1)
    pl.semaphore_wait(barrier, greeted)

    def remote(src, dst, send, recv, to):
        return pltpu.make_async_remote_copy(
            src_ref=src, dst_ref=dst, send_sem=send, recv_sem=recv, device_id=to, device_id_type=MESH
        )

    def send_own(j):
        return remote(raw.at[0, j], raw.at[2, j], d_send.at[0, j], d_recv.at[0, j], below)

    def forward(j):
        return remote(raw.at[2, j], raw.at[4, j], d_send.at[1, j], d_recv.at[1, j], below)

    def second(phase):
        return 3 - 2 * core if phase == 0 else 1 + 2 * core

    def passed(phase):
        return 2 if phase == 0 else 4 - 4 * core

    def sibling_second(phase):
        return 1 + 2 * core if phase == 0 else 3 - 2 * core

    def relay(phase, j):
        return remote(
            raw.at[passed(phase), j], raw.at[sibling_second(phase), j], r_send.at[phase, j], r_recv.at[phase, j], sibling
        )

    def relay_arrival(phase, j):
        return remote(raw.at[0, j], raw.at[second(phase), j], r_send.at[phase, j], r_recv.at[phase, j], sibling)

    def stats_send(phase):
        return remote(stats.at[2 * phase], stats.at[2 + 2 * phase], t_send.at[phase], t_recv.at[phase], below)

    def stats_relay(phase):
        return remote(
            stats.at[passed(phase)], stats.at[sibling_second(phase)], u_send.at[phase], u_recv.at[phase], sibling
        )

    def stats_relay_arrival(phase):
        return remote(stats.at[0], stats.at[second(phase)], u_send.at[phase], u_recv.at[phase], sibling)

    arrives = [has_above, has_above2]
    relays = [has_above, (core == 1) | has_above2]
    relayed = [has_above, (core == 0) | has_above2]

    for j in range(CHUNKS):
        load(j).wait()
        if j < CHUNKS // 2:

            @pl.when(has_below)
            def _():
                send_own(j).start()

    for j in range(CHUNKS):

        def add_up(n, totals):
            part = raw[0, j, pl.ds(pl.multiple_of(n * SLAB, SLAB), SLAB), :].astype(jnp.float32)
            return totals[0] + jnp.sum(part, axis=0, keepdims=True), totals[1] + jnp.sum(
                part * part, axis=0, keepdims=True
            )

        zero = jnp.zeros((1, WIDE), jnp.float32)
        first, squares = lax.fori_loop(0, rows // SLAB, add_up, (zero, zero))
        mom[j, 0:1, :] = first
        mom[j, 1:2, :] = squares
        mom[j, 2:8, :] = jnp.zeros((6, WIDE), jnp.float32)

    def moments_x(d):
        return remote(mom, mom_x.at[d - 1], m_send.at[d - 1], m_recv.at[d - 1], (v, 2 * x_peer(d) + zh))

    for d in (2, 1, 3):
        moments_x(d).start()
    for d in (1, 2, 3):
        moments_x(d).wait_recv()
    half_people = people // 2

    def half_scale(first, squares):
        average = first / half_people
        spread = jnp.maximum(squares / half_people - average * average, 0.0)
        return average, spread + 1e-06

    half_sums = (mom[...] + mom_x[1]) + (mom_x[0] + mom_x[2])
    average, spread = half_scale(half_sums[:, 0:1, :], half_sums[:, 1:2, :])
    stats[0, :, 0:1, :] = average
    stats[0, :, 1:2, :] = lax.rsqrt(spread)
    stats[0, :, 2:4, :] = half_sums[:, 0:2, :]
    stats[0, :, 4:8, :] = jnp.zeros((CHUNKS, 4, WIDE), jnp.float32)
    moments_z = remote(mom_z.at[0], mom_z.at[1], m_send.at[3], m_recv.at[3], opposite)

    @pl.when(has_below)
    def _():
        stats_send(0).start()
        for j in range(CHUNKS // 2, CHUNKS):
            send_own(j).start()

    line = positions[pl.ds(4 * v + x, 1), :]
    spots[...] = jnp.broadcast_to(line, (128, 128)).T

    def scale(slot, j, column):
        average = stats[slot, j, 0:1, :]
        inverse = stats[slot, j, 1:2, :]

        def body(n, carry):
            where = pl.ds(pl.multiple_of(n * SLAB, SLAB), SLAB)
            values = raw[slot, j, where, :].astype(jnp.float32)
            pair[where, pl.ds(column * WIDE, WIDE)] = ((values - average) * inverse).astype(jnp.bfloat16)
            return carry

        lax.fori_loop(0, rows // SLAB, body, 0)

    def turn(column, j):
        def body(n, carry):
            where = pl.ds(pl.multiple_of(n * SLAB, SLAB), SLAB)
            part = pair[where, pl.ds(column * WIDE, WIDE)]
            left[pl.ds(j * WIDE, WIDE), where] = part.T
            return carry

        lax.fori_loop(0, rows // SLAB, body, 0)

    def share_x(t, d):
        to = x_peer(d)
        return remote(
            partial.at[t, pl.ds(pl.multiple_of(to * 128, 128), 128)], from_x.at[t, d - 1],
            x_send.at[t, d - 1], x_recv.at[t, d - 1], (v, 2 * to + zh),
        )

    def share_z(t):
        return remote(to_z.at[t], from_z.at[t], z_send.at[t], z_recv.at[t], opposite)

    def multiply(t):
        partial[t] = jnp.dot(left[...], pair[...], preferred_element_type=jnp.float32).astype(jnp.bfloat16)
        for d in (2, 1, 3):
            share_x(t, d).start()

    def half(t, which):
        own = pl.ds(pl.multiple_of(x * 128 + which * 64, 64), 64)
        there = pl.ds(pl.multiple_of(which * 64, 64), 64)
        return (partial[t, own, :].astype(jnp.float32) + from_x[t, 1, there, :].astype(jnp.float32)) + (
            from_x[t, 0, there, :].astype(jnp.float32) + from_x[t, 2, there, :].astype(jnp.float32)
        )

    def reduce(t):
        for d in (1, 2, 3):
            share_x(t, d).wait_recv()
        to_z[t] = half(t, 1 - zh).astype(jnp.bfloat16)
        kept[t] = half(t, zh)

    def finish(t, first_slot, first_chunk, second_slot, second_chunk):
        share_z(t).wait_recv()
        half_rows = pl.ds(pl.multiple_of(zh * 64, 64), 64)
        own_spots = spots[half_rows, :]
        for column, slot, chunk in ((0, first_slot, first_chunk), (1, second_slot, second_chunk)):
            place = jnp.minimum(v + slot, blocks - 1) * CHUNKS + chunk
            inside = jnp.abs(positions[pl.ds(place, 1), :] - own_spots) <= WINDOW_BP
            usable = jnp.where(inside, partners[slot], -1) >= 0
            lanes = slice(column * WIDE, (column + 1) * WIDE)
            across = pl.ds(slot * CHUNKS + chunk, 1)
            mine = kept[t, :, lanes] * down[0, half_rows, :] * along[0, across, :]
            other = from_z[t, :, lanes].astype(jnp.float32) * down[1, half_rows, :] * along[1, across, :]
            total = (mine + other) / people + down[2, half_rows, :] * along[2, across, :]
            out[slot, chunk] = jnp.where(usable, total, 0.0)

    def whole_statistics():
        average, spread = half_scale(mom_z[0, 0], mom_z[0, 1])
        other_spread = half_scale(mom_z[1, 0], mom_z[1, 1])[1]
        mean = (mom_z[0, 0] + mom_z[1, 0]) / people
        inverse = lax.rsqrt((mom_z[0, 1] + mom_z[1, 1]) / people - mean * mean + 1e-06)
        along[0] = spread * lax.rsqrt(spread) * inverse
        along[1] = other_spread * lax.rsqrt(other_spread) * inverse
        along[2] = (average - mean) * inverse
        for k in range(3):
            down[k] = jnp.broadcast_to(along[k, pl.ds(x, 1), :], (128, 128)).T

    for t in (1, 0):
        for column in range(2):
            scale(0, 2 * t + column, column)
            turn(column, 2 * t + column)
    multiply(0)
    for column in range(2):
        scale(0, 2 + column, column)
    multiply(1)
    reduce(0)

    for phase in range(2):

        @pl.when(arrives[phase])
        def _():
            stats_send(phase).wait_recv()

        if phase == 0:

            @pl.when(has_below & has_above)
            def _():
                stats_send(1).start()

        @pl.when(relays[phase])
        def _():
            stats_relay(phase).start()

        @pl.when(relayed[phase])
        def _():
            stats_relay_arrival(phase).wait_recv()

        if phase == 1:
            for slot in range(5):
                for j in range(CHUNKS):
                    for row in range(2):
                        mom_z[0, row, slot * CHUNKS + j : slot * CHUNKS + j + 1, :] = stats[
                            slot, j, 2 + row : 3 + row, :
                        ]
            mom_z[0, :, 20:24, :] = jnp.zeros((2, 4, WIDE), jnp.float32)

        def step(j, carry):
            @pl.when(arrives[phase])
            def _():
                (send_own if phase == 0 else forward)(j).wait_recv()

            if phase == 0:

                @pl.when(has_below & has_above)
                def _():
                    forward(j).start()

            @pl.when(relays[phase])
            def _():
                relay(phase, j).start()

            if phase == 1:

                @pl.when(j == 3)
                def _():
                    moments_z.start()

                    def held(u, carry):
                        share_z(u).start()
                        return carry

                    lax.fori_loop(0, 8, held, 0)

            scale(2 + 2 * phase, j, 0)

            @pl.when(relayed[phase])
            def _():
                relay_arrival(phase, j).wait_recv()

            scale(second(phase), j, 1)
            t = 2 + 4 * phase + j
            multiply(t)
            reduce(t - 1)
            if phase == 1:

                @pl.when(j == 3)
                def _():
                    share_z(t - 1).start()

            return carry

        lax.fori_loop(0, CHUNKS, step, 0)

    reduce(1 + 2 * CHUNKS)
    share_z(1 + 2 * CHUNKS).start()
    moments_z.wait_recv()
    whole_statistics()
    for t in range(2):
        finish(t, 0, 2 * t, 0, 2 * t + 1)
    for phase in range(2):

        def last(j, carry):
            finish(2 + 4 * phase + j, 2 + 2 * phase, j, second(phase), j)
            return carry

        lax.fori_loop(0, CHUNKS, last, 0)

    for d in (1, 2, 3):
        moments_x(d).wait_send()
    moments_z.wait_send()

    @pl.when(has_below)
    def _():
        stats_send(0).wait_send()

    @pl.when(has_below & has_above)
    def _():
        stats_send(1).wait_send()

    for phase in range(2):

        @pl.when(relays[phase])
        def _():
            stats_relay(phase).wait_send()

    def drain(j, carry):
        @pl.when(has_below)
        def _():
            send_own(j).wait_send()

        @pl.when(has_below & has_above)
        def _():
            forward(j).wait_send()

        for phase in range(2):

            @pl.when(relays[phase])
            def _():
                relay(phase, j).wait_send()

        return carry

    lax.fori_loop(0, CHUNKS, drain, 0)

    def drain_sums(t, carry):
        for d in (1, 2, 3):
            share_x(t, d).wait_send()
        share_z(t).wait_send()
        return carry

    lax.fori_loop(0, 2 + 2 * CHUNKS, drain_sums, 0)


def tiles(dosage, positions, partners):
    rows, width = dosage.shape
    steps = 2 + 2 * CHUNKS
    dma = pltpu.SemaphoreType.DMA
    return pl.pallas_call(
        kernel,
        out_shape=jax.ShapeDtypeStruct((5, CHUNKS, 64, WIDE), jnp.float32),
        in_specs=[
            pl.BlockSpec(memory_space=pl.ANY),
            pl.BlockSpec(memory_space=pltpu.VMEM),
            pl.BlockSpec(memory_space=pltpu.SMEM),
        ],
        out_specs=pl.BlockSpec(memory_space=pltpu.VMEM),
        scratch_shapes=[
            pltpu.VMEM((5, CHUNKS, rows, WIDE), jnp.bfloat16),
            pltpu.VMEM((5, CHUNKS, 8, WIDE), jnp.float32),
            pltpu.VMEM((width, rows), jnp.bfloat16),
            pltpu.VMEM((rows, 2 * WIDE), jnp.bfloat16),
            pltpu.VMEM((steps, width, 2 * WIDE), jnp.bfloat16),
            pltpu.VMEM((steps, 3, 128, 2 * WIDE), jnp.bfloat16),
            pltpu.VMEM((steps, 64, 2 * WIDE), jnp.bfloat16),
            pltpu.VMEM((steps, 64, 2 * WIDE), jnp.float32),
            pltpu.VMEM((steps, 64, 2 * WIDE), jnp.bfloat16),
            pltpu.VMEM((CHUNKS, 8, WIDE), jnp.float32),
            pltpu.VMEM((3, CHUNKS, 8, WIDE), jnp.float32),
            pltpu.VMEM((2, 2, 24, WIDE), jnp.float32),
            pltpu.VMEM((128, 128), jnp.int32),
            pltpu.VMEM((3, 24, WIDE), jnp.float32),
            pltpu.VMEM((3, 128, 128), jnp.float32),
            dma((CHUNKS,)),
            dma((2, CHUNKS)), dma((2, CHUNKS)), dma((2, CHUNKS)), dma((2, CHUNKS)),
            dma((2,)), dma((2,)), dma((2,)), dma((2,)),
            dma((4,)), dma((4,)),
            dma((steps, 3)), dma((steps, 3)), dma((steps,)), dma((steps,)),
        ],
        compiler_params=pltpu.CompilerParams(
            collective_id=0, has_side_effects=True, vmem_limit_bytes=60 * 2**20
        ),
    )(dosage, positions.reshape(-1, WIDE), partners)


def per_device(dosage, positions, partners):
    masked = tiles(dosage, positions, partners)
    share_rows = masked.shape[2]
    return masked.transpose(2, 0, 1, 3).reshape(share_rows, partners.shape[0], dosage.shape[1]).astype(jnp.bfloat16)


def solution(mesh):
    return jax.shard_map(
        per_device,
        mesh=mesh,
        in_specs=(P("ind", "var"), P(), P("var")),
        out_specs=P("ind", "var", None),
        check_vma=False,
    )
```

```python
import jax
import jax.numpy as jnp
from jax import lax
from jax.experimental import pallas as pl
from jax.experimental.pallas import tpu as pltpu
from jax.sharding import PartitionSpec as P

WINDOW_BP = 3000000
MESH = pl.DeviceIdType.MESH

CHUNKS = 4
WIDE = 128
SLAB = 256


def kernel(
    dosage, positions, partners, out, raw, stats, left, pair, partial, from_x, to_z, kept, from_z, mom, mom_x, mom_z, spots, along, down,
    load_sem, d_send, d_recv, r_send, r_recv, t_send, t_recv, u_send, u_recv,
    m_send, m_recv, x_send, x_recv, z_send, z_recv,
):
    v, i = lax.axis_index("var"), lax.axis_index("ind")
    rows = dosage.shape[0]
    blocks = lax.axis_size("var")
    people = rows * lax.axis_size("ind")
    core = lax.rem(v, 2)
    x, zh = lax.div(i, 2), lax.rem(i, 2)
    below = (jnp.maximum(v - 2, 0), i)
    above = (jnp.minimum(v + 2, blocks - 1), i)
    sibling = (v + 1 - 2 * core, i)
    opposite = (v, i + 1 - 2 * zh)

    def x_peer(d):
        return lax.rem(x + d, 4)

    has_below, has_above, has_above2 = v >= 2, v + 2 < blocks, lax.div(v, 2) + 2 < lax.div(blocks, 2)

    barrier = pltpu.get_barrier_semaphore()
    for d in (1, 2, 3):
        pl.semaphore_signal(barrier, inc=1, device_id=(v, 2 * x_peer(d) + zh), device_id_type=MESH)
    pl.semaphore_signal(barrier, inc=1, device_id=sibling, device_id_type=MESH)
    pl.semaphore_signal(barrier, inc=1, device_id=opposite, device_id_type=MESH)

    @pl.when(has_below)
    def _():
        pl.semaphore_signal(barrier, inc=1, device_id=below, device_id_type=MESH)

    @pl.when(has_above)
    def _():
        pl.semaphore_signal(barrier, inc=1, device_id=above, device_id_type=MESH)

    def load(j):
        return pltpu.make_async_copy(dosage.at[:, pl.ds(j * WIDE, WIDE)], raw.at[0, j], load_sem.at[j])

    for j in range(CHUNKS):
        load(j).start()

    greeted = 5 + jnp.minimum(lax.div(v, 2), 1) + jnp.minimum(lax.div(blocks - 1 - v, 2), 1)
    pl.semaphore_wait(barrier, greeted)

    def remote(src, dst, send, recv, to):
        return pltpu.make_async_remote_copy(
            src_ref=src, dst_ref=dst, send_sem=send, recv_sem=recv, device_id=to, device_id_type=MESH
        )

    def send_own(j):
        return remote(raw.at[0, j], raw.at[2, j], d_send.at[0, j], d_recv.at[0, j], below)

    def forward(j):
        return remote(raw.at[2, j], raw.at[4, j], d_send.at[1, j], d_recv.at[1, j], below)

    def second(phase):
        return 3 - 2 * core if phase == 0 else 1 + 2 * core

    def passed(phase):
        return 2 if phase == 0 else 4 - 4 * core

    def sibling_second(phase):
        return 1 + 2 * core if phase == 0 else 3 - 2 * core

    def relay(phase, j):
        return remote(
            raw.at[passed(phase), j], raw.at[sibling_second(phase), j], r_send.at[phase, j], r_recv.at[phase, j], sibling
        )

    def relay_arrival(phase, j):
        return remote(raw.at[0, j], raw.at[second(phase), j], r_send.at[phase, j], r_recv.at[phase, j], sibling)

    def stats_send(phase):
        return remote(stats.at[2 * phase], stats.at[2 + 2 * phase], t_send.at[phase], t_recv.at[phase], below)

    def stats_relay(phase):
        return remote(
            stats.at[passed(phase)], stats.at[sibling_second(phase)], u_send.at[phase], u_recv.at[phase], sibling
        )

    def stats_relay_arrival(phase):
        return remote(stats.at[0], stats.at[second(phase)], u_send.at[phase], u_recv.at[phase], sibling)

    arrives = [has_above, has_above2]
    relays = [has_above, (core == 1) | has_above2]
    relayed = [has_above, (core == 0) | has_above2]

    for j in range(CHUNKS):
        load(j).wait()
        if j < CHUNKS // 2:

            @pl.when(has_below)
            def _():
                send_own(j).start()

    for j in range(CHUNKS):

        def add_up(n, totals):
            part = raw[0, j, pl.ds(pl.multiple_of(n * SLAB, SLAB), SLAB), :].astype(jnp.float32)
            return totals[0] + jnp.sum(part, axis=0, keepdims=True), totals[1] + jnp.sum(
                part * part, axis=0, keepdims=True
            )

        zero = jnp.zeros((1, WIDE), jnp.float32)
        first, squares = lax.fori_loop(0, rows // SLAB, add_up, (zero, zero))
        mom[j, 0:1, :] = first
        mom[j, 1:2, :] = squares
        mom[j, 2:8, :] = jnp.zeros((6, WIDE), jnp.float32)

    def moments_x(d):
        return remote(mom, mom_x.at[d - 1], m_send.at[d - 1], m_recv.at[d - 1], (v, 2 * x_peer(d) + zh))

    for d in (2, 1, 3):
        moments_x(d).start()
    for d in (1, 2, 3):
        moments_x(d).wait_recv()
    half_people = people // 2

    def half_scale(first, squares):
        average = first / half_people
        spread = jnp.maximum(squares / half_people - average * average, 0.0)
        return average, spread + 1e-06

    half_sums = (mom[...] + mom_x[1]) + (mom_x[0] + mom_x[2])
    average, spread = half_scale(half_sums[:, 0:1, :], half_sums[:, 1:2, :])
    stats[0, :, 0:1, :] = average
    stats[0, :, 1:2, :] = lax.rsqrt(spread)
    stats[0, :, 2:4, :] = half_sums[:, 0:2, :]
    stats[0, :, 4:8, :] = jnp.zeros((CHUNKS, 4, WIDE), jnp.float32)
    moments_z = remote(mom_z.at[0, x], mom_z.at[1, x], m_send.at[3], m_recv.at[3], opposite)

    def moments_back(d):
        return remote(
            mom_z.at[1, x], mom_z.at[1, x], m_send.at[3 + d], m_recv.at[3 + d], (v, 2 * x_peer(d) + zh)
        )

    def moments_back_arrival(d):
        there = mom_z.at[1, x_peer(4 - d)]
        return remote(there, there, m_send.at[3 + d], m_recv.at[3 + d], (v, 2 * x_peer(d) + zh))


    @pl.when(has_below)
    def _():
        stats_send(0).start()
        for j in range(CHUNKS // 2, CHUNKS):
            send_own(j).start()

    line = positions[pl.ds(4 * v + x, 1), :]
    spots[...] = jnp.broadcast_to(line, (128, 128)).T

    def scale(slot, j, column):
        average = stats[slot, j, 0:1, :]
        inverse = stats[slot, j, 1:2, :]

        def body(n, carry):
            where = pl.ds(pl.multiple_of(n * SLAB, SLAB), SLAB)
            values = raw[slot, j, where, :].astype(jnp.float32)
            pair[where, pl.ds(column * WIDE, WIDE)] = ((values - average) * inverse).astype(jnp.bfloat16)
            return carry

        lax.fori_loop(0, rows // SLAB, body, 0)

    def turn(column, j):
        def body(n, carry):
            where = pl.ds(pl.multiple_of(n * SLAB, SLAB), SLAB)
            part = pair[where, pl.ds(column * WIDE, WIDE)]
            left[pl.ds(j * WIDE, WIDE), where] = part.T
            return carry

        lax.fori_loop(0, rows // SLAB, body, 0)

    def share_x(t, d):
        to = x_peer(d)
        return remote(
            partial.at[t, pl.ds(pl.multiple_of(to * 128, 128), 128)], from_x.at[t, d - 1],
            x_send.at[t, d - 1], x_recv.at[t, d - 1], (v, 2 * to + zh),
        )

    def share_z(t):
        return remote(to_z.at[t], from_z.at[t], z_send.at[t], z_recv.at[t], opposite)

    def multiply(t):
        partial[t] = jnp.dot(left[...], pair[...], preferred_element_type=jnp.float32).astype(jnp.bfloat16)
        for d in (2, 1, 3):
            share_x(t, d).start()

    def half(t, which):
        own = pl.ds(pl.multiple_of(x * 128 + which * 64, 64), 64)
        there = pl.ds(pl.multiple_of(which * 64, 64), 64)
        return (partial[t, own, :].astype(jnp.float32) + from_x[t, 1, there, :].astype(jnp.float32)) + (
            from_x[t, 0, there, :].astype(jnp.float32) + from_x[t, 2, there, :].astype(jnp.float32)
        )

    def reduce(t):
        for d in (1, 2, 3):
            share_x(t, d).wait_recv()
        to_z[t] = half(t, 1 - zh).astype(jnp.bfloat16)
        kept[t] = half(t, zh)

    def finish(t, first_slot, first_chunk, second_slot, second_chunk):
        share_z(t).wait_recv()
        half_rows = pl.ds(pl.multiple_of(zh * 64, 64), 64)
        own_spots = spots[half_rows, :]
        for column, slot, chunk in ((0, first_slot, first_chunk), (1, second_slot, second_chunk)):
            place = jnp.minimum(v + slot, blocks - 1) * CHUNKS + chunk
            inside = jnp.abs(positions[pl.ds(place, 1), :] - own_spots) <= WINDOW_BP
            usable = jnp.where(inside, partners[slot], -1) >= 0
            lanes = slice(column * WIDE, (column + 1) * WIDE)
            across = pl.ds(slot, 1)
            mine = kept[t, :, lanes] * down[0, half_rows, :] * along[0, chunk, across, :]
            other = from_z[t, :, lanes].astype(jnp.float32) * down[1, half_rows, :] * along[1, chunk, across, :]
            total = (mine + other) / people + down[2, half_rows, :] * along[2, chunk, across, :]
            out[slot, chunk] = jnp.where(usable, total, 0.0)

    def whole_statistics():
        average, spread = half_scale(mom_z[0, :, 0], mom_z[0, :, 1])
        other_spread = half_scale(mom_z[1, :, 0], mom_z[1, :, 1])[1]
        mean = (mom_z[0, :, 0] + mom_z[1, :, 0]) / people
        inverse = lax.rsqrt((mom_z[0, :, 1] + mom_z[1, :, 1]) / people - mean * mean + 1e-06)
        along[0] = spread * lax.rsqrt(spread) * inverse
        along[1] = other_spread * lax.rsqrt(other_spread) * inverse
        along[2] = (average - mean) * inverse
        for k in range(3):
            down[k] = jnp.broadcast_to(along[k, x, 0:1, :], (128, 128)).T

    for t in (1, 0):
        for column in range(2):
            scale(0, 2 * t + column, column)
            turn(column, 2 * t + column)
    multiply(0)
    for column in range(2):
        scale(0, 2 + column, column)
    multiply(1)
    reduce(0)

    for phase in range(2):

        @pl.when(arrives[phase])
        def _():
            stats_send(phase).wait_recv()

        if phase == 0:

            @pl.when(has_below & has_above)
            def _():
                stats_send(1).start()

        @pl.when(relays[phase])
        def _():
            stats_relay(phase).start()

        @pl.when(relayed[phase])
        def _():
            stats_relay_arrival(phase).wait_recv()

        if phase == 1:
            for slot in range(5):
                for j in range(CHUNKS):
                    for row in range(2):
                        mom_z[0, j, row, slot : slot + 1, :] = stats[slot, j, 2 + row : 3 + row, :]
            mom_z[0, :, :, 5:8, :] = jnp.zeros((CHUNKS, 2, 3, WIDE), jnp.float32)

        def step(j, carry):
            @pl.when(arrives[phase])
            def _():
                (send_own if phase == 0 else forward)(j).wait_recv()

            if phase == 0:

                @pl.when(has_below & has_above)
                def _():
                    forward(j).start()

            @pl.when(relays[phase])
            def _():
                relay(phase, j).start()

            if phase == 1:

                @pl.when(j == 3)
                def _():
                    moments_z.start()

                    def held(u, carry):
                        share_z(u).start()
                        return carry

                    lax.fori_loop(0, 8, held, 0)

            scale(2 + 2 * phase, j, 0)

            @pl.when(relayed[phase])
            def _():
                relay_arrival(phase, j).wait_recv()

            scale(second(phase), j, 1)
            t = 2 + 4 * phase + j
            multiply(t)
            reduce(t - 1)
            if phase == 1:

                @pl.when(j == 3)
                def _():
                    share_z(t - 1).start()

            return carry

        lax.fori_loop(0, CHUNKS, step, 0)

    reduce(1 + 2 * CHUNKS)
    share_z(1 + 2 * CHUNKS).start()
    moments_z.wait_recv()
    for d in (1, 2, 3):
        moments_back(d).start()
    for d in (1, 2, 3):
        moments_back_arrival(d).wait_recv()
    whole_statistics()
    for t in range(2):
        finish(t, 0, 2 * t, 0, 2 * t + 1)
    for phase in range(2):

        def last(j, carry):
            finish(2 + 4 * phase + j, 2 + 2 * phase, j, second(phase), j)
            return carry

        lax.fori_loop(0, CHUNKS, last, 0)

    for d in (1, 2, 3):
        moments_x(d).wait_send()
    moments_z.wait_send()
    for d in (1, 2, 3):
        moments_back(d).wait_send()

    @pl.when(has_below)
    def _():
        stats_send(0).wait_send()

    @pl.when(has_below & has_above)
    def _():
        stats_send(1).wait_send()

    for phase in range(2):

        @pl.when(relays[phase])
        def _():
            stats_relay(phase).wait_send()

    def drain(j, carry):
        @pl.when(has_below)
        def _():
            send_own(j).wait_send()

        @pl.when(has_below & has_above)
        def _():
            forward(j).wait_send()

        for phase in range(2):

            @pl.when(relays[phase])
            def _():
                relay(phase, j).wait_send()

        return carry

    lax.fori_loop(0, CHUNKS, drain, 0)

    def drain_sums(t, carry):
        for d in (1, 2, 3):
            share_x(t, d).wait_send()
        share_z(t).wait_send()
        return carry

    lax.fori_loop(0, 2 + 2 * CHUNKS, drain_sums, 0)


def tiles(dosage, positions, partners):
    rows, width = dosage.shape
    steps = 2 + 2 * CHUNKS
    dma = pltpu.SemaphoreType.DMA
    return pl.pallas_call(
        kernel,
        out_shape=jax.ShapeDtypeStruct((5, CHUNKS, 64, WIDE), jnp.float32),
        in_specs=[
            pl.BlockSpec(memory_space=pl.ANY),
            pl.BlockSpec(memory_space=pltpu.VMEM),
            pl.BlockSpec(memory_space=pltpu.SMEM),
        ],
        out_specs=pl.BlockSpec(memory_space=pltpu.VMEM),
        scratch_shapes=[
            pltpu.VMEM((5, CHUNKS, rows, WIDE), jnp.bfloat16),
            pltpu.VMEM((5, CHUNKS, 8, WIDE), jnp.float32),
            pltpu.VMEM((width, rows), jnp.bfloat16),
            pltpu.VMEM((rows, 2 * WIDE), jnp.bfloat16),
            pltpu.VMEM((steps, width, 2 * WIDE), jnp.bfloat16),
            pltpu.VMEM((steps, 3, 128, 2 * WIDE), jnp.bfloat16),
            pltpu.VMEM((steps, 64, 2 * WIDE), jnp.bfloat16),
            pltpu.VMEM((steps, 64, 2 * WIDE), jnp.float32),
            pltpu.VMEM((steps, 64, 2 * WIDE), jnp.bfloat16),
            pltpu.VMEM((CHUNKS, 8, WIDE), jnp.float32),
            pltpu.VMEM((3, CHUNKS, 8, WIDE), jnp.float32),
            pltpu.VMEM((2, CHUNKS, 2, 8, WIDE), jnp.float32),
            pltpu.VMEM((128, 128), jnp.int32),
            pltpu.VMEM((3, CHUNKS, 8, WIDE), jnp.float32),
            pltpu.VMEM((3, 128, 128), jnp.float32),
            dma((CHUNKS,)),
            dma((2, CHUNKS)), dma((2, CHUNKS)), dma((2, CHUNKS)), dma((2, CHUNKS)),
            dma((2,)), dma((2,)), dma((2,)), dma((2,)),
            dma((7,)), dma((7,)),
            dma((steps, 3)), dma((steps, 3)), dma((steps,)), dma((steps,)),
        ],
        compiler_params=pltpu.CompilerParams(
            collective_id=0, has_side_effects=True, vmem_limit_bytes=60 * 2**20
        ),
    )(dosage, positions.reshape(-1, WIDE), partners)


def per_device(dosage, positions, partners):
    masked = tiles(dosage, positions, partners)
    share_rows = masked.shape[2]
    return masked.transpose(2, 0, 1, 3).reshape(share_rows, partners.shape[0], dosage.shape[1]).astype(jnp.bfloat16)


def solution(mesh):
    return jax.shard_map(
        per_device,
        mesh=mesh,
        in_specs=(P("ind", "var"), P(), P("var")),
        out_specs=P("ind", "var", None),
        check_vma=False,
    )
```

```python
import jax
import jax.numpy as jnp
from jax import lax
from jax.experimental import pallas as pl
from jax.experimental.pallas import tpu as pltpu
from jax.sharding import PartitionSpec as P

WINDOW_BP = 3000000
MESH = pl.DeviceIdType.MESH

CHUNKS = 4
WIDE = 128
SLAB = 256


def kernel(
    dosage, positions, partners, out, raw, stats, left, pair, partial, from_x, to_z, kept, from_z, mom, mom_x, mom_z, spots, along, down,
    load_sem, d_send, d_recv, r_send, r_recv, t_send, t_recv, u_send, u_recv,
    m_send, m_recv, x_send, x_recv, z_send, z_recv, go,
):
    v, i = lax.axis_index("var"), lax.axis_index("ind")
    rows = dosage.shape[0]
    blocks = lax.axis_size("var")
    people = rows * lax.axis_size("ind")
    core = lax.rem(v, 2)
    x, zh = lax.div(i, 2), lax.rem(i, 2)
    below = (jnp.maximum(v - 2, 0), i)
    above = (jnp.minimum(v + 2, blocks - 1), i)
    sibling = (v + 1 - 2 * core, i)
    opposite = (v, i + 1 - 2 * zh)

    def x_peer(d):
        return lax.rem(x + d, 4)

    has_below, has_above, has_above2 = v >= 2, v + 2 < blocks, lax.div(v, 2) + 2 < lax.div(blocks, 2)

    chip, chips = lax.div(v, 2), lax.div(blocks, 2)

    barrier = pltpu.get_barrier_semaphore()
    for d in (1, 2, 3):
        pl.semaphore_signal(barrier, inc=1, device_id=(v, 2 * x_peer(d) + zh), device_id_type=MESH)
    pl.semaphore_signal(barrier, inc=1, device_id=sibling, device_id_type=MESH)
    pl.semaphore_signal(barrier, inc=1, device_id=opposite, device_id_type=MESH)

    @pl.when(has_below)
    def _():
        pl.semaphore_signal(barrier, inc=1, device_id=below, device_id_type=MESH)

    @pl.when(has_above)
    def _():
        pl.semaphore_signal(barrier, inc=1, device_id=above, device_id_type=MESH)

    def load(j):
        return pltpu.make_async_copy(dosage.at[:, pl.ds(j * WIDE, WIDE)], raw.at[0, j], load_sem.at[j])

    for j in range(CHUNKS):
        load(j).start()

    greeted = 5 + jnp.minimum(lax.div(v, 2), 1) + jnp.minimum(lax.div(blocks - 1 - v, 2), 1)
    pl.semaphore_wait(barrier, greeted)

    def remote(src, dst, send, recv, to):
        return pltpu.make_async_remote_copy(
            src_ref=src, dst_ref=dst, send_sem=send, recv_sem=recv, device_id=to, device_id_type=MESH
        )

    def send_own(j):
        return remote(raw.at[0, j], raw.at[2, j], d_send.at[0, j], d_recv.at[0, j], below)

    def forward(j):
        return remote(raw.at[2, j], raw.at[4, j], d_send.at[1, j], d_recv.at[1, j], below)

    def second(phase):
        return 3 - 2 * core if phase == 0 else 1 + 2 * core

    def passed(phase):
        return 2 if phase == 0 else 4 - 4 * core

    def sibling_second(phase):
        return 1 + 2 * core if phase == 0 else 3 - 2 * core

    def relay(phase, j):
        return remote(
            raw.at[passed(phase), j], raw.at[sibling_second(phase), j], r_send.at[phase, j], r_recv.at[phase, j], sibling
        )

    def relay_arrival(phase, j):
        return remote(raw.at[0, j], raw.at[second(phase), j], r_send.at[phase, j], r_recv.at[phase, j], sibling)

    def stats_send(phase):
        return remote(stats.at[2 * phase], stats.at[2 + 2 * phase], t_send.at[phase], t_recv.at[phase], below)

    def stats_relay(phase):
        return remote(
            stats.at[passed(phase)], stats.at[sibling_second(phase)], u_send.at[phase], u_recv.at[phase], sibling
        )

    def stats_relay_arrival(phase):
        return remote(stats.at[0], stats.at[second(phase)], u_send.at[phase], u_recv.at[phase], sibling)

    arrives = [has_above, has_above2]
    relays = [has_above, (core == 1) | has_above2]
    relayed = [has_above, (core == 0) | has_above2]

    for j in range(CHUNKS):
        load(j).wait()
        if j < CHUNKS // 2:

            @pl.when(has_below)
            def _():
                send_own(j).start()

    for j in range(CHUNKS):

        def add_up(n, totals):
            part = raw[0, j, pl.ds(pl.multiple_of(n * SLAB, SLAB), SLAB), :].astype(jnp.float32)
            return totals[0] + jnp.sum(part, axis=0, keepdims=True), totals[1] + jnp.sum(
                part * part, axis=0, keepdims=True
            )

        zero = jnp.zeros((1, WIDE), jnp.float32)
        first, squares = lax.fori_loop(0, rows // SLAB, add_up, (zero, zero))
        mom[j, 0:1, :] = first
        mom[j, 1:2, :] = squares
        mom[j, 2:8, :] = jnp.zeros((6, WIDE), jnp.float32)

    def moments_x(d):
        return remote(mom, mom_x.at[d - 1], m_send.at[d - 1], m_recv.at[d - 1], (v, 2 * x_peer(d) + zh))

    for d in (2, 1, 3):
        moments_x(d).start()
    for d in (1, 2, 3):
        moments_x(d).wait_recv()
    half_people = people // 2

    def half_scale(first, squares):
        average = first / half_people
        spread = jnp.maximum(squares / half_people - average * average, 0.0)
        return average, spread + 1e-06

    half_sums = (mom[...] + mom_x[1]) + (mom_x[0] + mom_x[2])
    average, spread = half_scale(half_sums[:, 0:1, :], half_sums[:, 1:2, :])
    stats[0, :, 0:1, :] = average
    stats[0, :, 1:2, :] = lax.rsqrt(spread)
    stats[0, :, 2:4, :] = half_sums[:, 0:2, :]
    stats[0, :, 4:8, :] = jnp.zeros((CHUNKS, 4, WIDE), jnp.float32)
    moments_z = remote(mom_z.at[0, x], mom_z.at[1, x], m_send.at[3], m_recv.at[3], opposite)

    def moments_back(d):
        return remote(
            mom_z.at[1, x], mom_z.at[1, x], m_send.at[3 + d], m_recv.at[3 + d], (v, 2 * x_peer(d) + zh)
        )

    def moments_back_arrival(d):
        there = mom_z.at[1, x_peer(4 - d)]
        return remote(there, there, m_send.at[3 + d], m_recv.at[3 + d], (v, 2 * x_peer(d) + zh))


    @pl.when(has_below)
    def _():
        stats_send(0).start()
        for j in range(CHUNKS // 2, CHUNKS):
            send_own(j).start()

    line = positions[pl.ds(4 * v + x, 1), :]
    spots[...] = jnp.broadcast_to(line, (128, 128)).T

    def scale(slot, j, column):
        average = stats[slot, j, 0:1, :]
        inverse = stats[slot, j, 1:2, :]

        def body(n, carry):
            where = pl.ds(pl.multiple_of(n * SLAB, SLAB), SLAB)
            values = raw[slot, j, where, :].astype(jnp.float32)
            pair[where, pl.ds(column * WIDE, WIDE)] = ((values - average) * inverse).astype(jnp.bfloat16)
            return carry

        lax.fori_loop(0, rows // SLAB, body, 0)

    def turn(column, j):
        def body(n, carry):
            where = pl.ds(pl.multiple_of(n * SLAB, SLAB), SLAB)
            part = pair[where, pl.ds(column * WIDE, WIDE)]
            left[pl.ds(j * WIDE, WIDE), where] = part.T
            return carry

        lax.fori_loop(0, rows // SLAB, body, 0)

    def share_x(t, d):
        to = x_peer(d)
        return remote(
            partial.at[t, pl.ds(pl.multiple_of(to * 128, 128), 128)], from_x.at[t, d - 1],
            x_send.at[t, d - 1], x_recv.at[t, d - 1], (v, 2 * to + zh),
        )

    def share_z(t):
        return remote(to_z.at[t], from_z.at[t], z_send.at[t], z_recv.at[t], opposite)

    def multiply(t):
        partial[t] = jnp.dot(left[...], pair[...], preferred_element_type=jnp.float32).astype(jnp.bfloat16)
        for d in (2, 1, 3):
            share_x(t, d).start()

    def half(t, which):
        own = pl.ds(pl.multiple_of(x * 128 + which * 64, 64), 64)
        there = pl.ds(pl.multiple_of(which * 64, 64), 64)
        return (partial[t, own, :].astype(jnp.float32) + from_x[t, 1, there, :].astype(jnp.float32)) + (
            from_x[t, 0, there, :].astype(jnp.float32) + from_x[t, 2, there, :].astype(jnp.float32)
        )

    def reduce(t):
        for d in (1, 2, 3):
            share_x(t, d).wait_recv()
        to_z[t] = half(t, 1 - zh).astype(jnp.bfloat16)
        kept[t] = half(t, zh)

    def finish(t, first_slot, first_chunk, second_slot, second_chunk):
        share_z(t).wait_recv()
        half_rows = pl.ds(pl.multiple_of(zh * 64, 64), 64)
        own_spots = spots[half_rows, :]
        for column, slot, chunk in ((0, first_slot, first_chunk), (1, second_slot, second_chunk)):
            place = jnp.minimum(v + slot, blocks - 1) * CHUNKS + chunk
            inside = jnp.abs(positions[pl.ds(place, 1), :] - own_spots) <= WINDOW_BP
            usable = jnp.where(inside, partners[slot], -1) >= 0
            lanes = slice(column * WIDE, (column + 1) * WIDE)
            across = pl.ds(slot, 1)
            mine = kept[t, :, lanes] * down[0, half_rows, :] * along[0, chunk, across, :]
            other = from_z[t, :, lanes].astype(jnp.float32) * down[1, half_rows, :] * along[1, chunk, across, :]
            total = (mine + other) / people + down[2, half_rows, :] * along[2, chunk, across, :]
            out[slot, chunk] = jnp.where(usable, total, 0.0)

    def whole_statistics():
        average, spread = half_scale(mom_z[0, :, 0], mom_z[0, :, 1])
        other_spread = half_scale(mom_z[1, :, 0], mom_z[1, :, 1])[1]
        mean = (mom_z[0, :, 0] + mom_z[1, :, 0]) / people
        inverse = lax.rsqrt((mom_z[0, :, 1] + mom_z[1, :, 1]) / people - mean * mean + 1e-06)
        along[0] = spread * lax.rsqrt(spread) * inverse
        along[1] = other_spread * lax.rsqrt(other_spread) * inverse
        along[2] = (average - mean) * inverse
        for k in range(3):
            down[k] = jnp.broadcast_to(along[k, x, 0:1, :], (128, 128)).T

    for t in (1, 0):
        for column in range(2):
            scale(0, 2 * t + column, column)
            turn(column, 2 * t + column)
    multiply(0)
    for column in range(2):
        scale(0, 2 + column, column)
    multiply(1)
    reduce(0)

    for phase in range(2):

        @pl.when(arrives[phase])
        def _():
            stats_send(phase).wait_recv()

        if phase == 0:

            @pl.when(has_below & has_above)
            def _():
                stats_send(1).start()

        @pl.when(relays[phase])
        def _():
            stats_relay(phase).start()

        @pl.when(relayed[phase])
        def _():
            stats_relay_arrival(phase).wait_recv()

        if phase == 1:
            for slot in range(5):
                for j in range(CHUNKS):
                    for row in range(2):
                        mom_z[0, j, row, slot : slot + 1, :] = stats[slot, j, 2 + row : 3 + row, :]
            mom_z[0, :, :, 5:8, :] = jnp.zeros((CHUNKS, 2, 3, WIDE), jnp.float32)

        def step(j, carry):
            @pl.when(arrives[phase])
            def _():
                (send_own if phase == 0 else forward)(j).wait_recv()

            if phase == 0:

                @pl.when(has_below & has_above)
                def _():
                    forward(j).start()

            @pl.when(relays[phase])
            def _():
                relay(phase, j).start()

            if phase == 1:

                @pl.when(j == 3)
                def _():
                    @pl.when(chip + 2 >= chips)
                    def _():
                        pl.semaphore_wait(go, 1)

                    @pl.when((chip + 3 >= chips) & has_above)
                    def _():
                        pl.semaphore_signal(go, inc=1, device_id=above, device_id_type=MESH)

                    moments_z.start()

                    def held(u, carry):
                        share_z(u).start()
                        return carry

                    lax.fori_loop(0, 8, held, 0)

            scale(2 + 2 * phase, j, 0)

            @pl.when(relayed[phase])
            def _():
                relay_arrival(phase, j).wait_recv()

            scale(second(phase), j, 1)
            t = 2 + 4 * phase + j
            multiply(t)
            reduce(t - 1)
            if phase == 1:

                @pl.when(j == 3)
                def _():
                    share_z(t - 1).start()

            return carry

        lax.fori_loop(0, CHUNKS, step, 0)

    reduce(1 + 2 * CHUNKS)
    share_z(1 + 2 * CHUNKS).start()
    moments_z.wait_recv()
    for d in (1, 2, 3):
        moments_back(d).start()
    for d in (1, 2, 3):
        moments_back_arrival(d).wait_recv()
    whole_statistics()
    for t in range(2):
        finish(t, 0, 2 * t, 0, 2 * t + 1)
    for phase in range(2):

        def last(j, carry):
            finish(2 + 4 * phase + j, 2 + 2 * phase, j, second(phase), j)
            return carry

        lax.fori_loop(0, CHUNKS, last, 0)

    for d in (1, 2, 3):
        moments_x(d).wait_send()
    moments_z.wait_send()
    for d in (1, 2, 3):
        moments_back(d).wait_send()

    @pl.when(has_below)
    def _():
        stats_send(0).wait_send()

    @pl.when(has_below & has_above)
    def _():
        stats_send(1).wait_send()

    for phase in range(2):

        @pl.when(relays[phase])
        def _():
            stats_relay(phase).wait_send()

    def drain(j, carry):
        @pl.when(has_below)
        def _():
            send_own(j).wait_send()

        @pl.when(has_below & has_above)
        def _():
            forward(j).wait_send()

        for phase in range(2):

            @pl.when(relays[phase])
            def _():
                relay(phase, j).wait_send()

        return carry

    lax.fori_loop(0, CHUNKS, drain, 0)

    def drain_sums(t, carry):
        for d in (1, 2, 3):
            share_x(t, d).wait_send()
        share_z(t).wait_send()
        return carry

    lax.fori_loop(0, 2 + 2 * CHUNKS, drain_sums, 0)


def tiles(dosage, positions, partners):
    rows, width = dosage.shape
    steps = 2 + 2 * CHUNKS
    dma = pltpu.SemaphoreType.DMA
    return pl.pallas_call(
        kernel,
        out_shape=jax.ShapeDtypeStruct((5, CHUNKS, 64, WIDE), jnp.float32),
        in_specs=[
            pl.BlockSpec(memory_space=pl.ANY),
            pl.BlockSpec(memory_space=pltpu.VMEM),
            pl.BlockSpec(memory_space=pltpu.SMEM),
        ],
        out_specs=pl.BlockSpec(memory_space=pltpu.VMEM),
        scratch_shapes=[
            pltpu.VMEM((5, CHUNKS, rows, WIDE), jnp.bfloat16),
            pltpu.VMEM((5, CHUNKS, 8, WIDE), jnp.float32),
            pltpu.VMEM((width, rows), jnp.bfloat16),
            pltpu.VMEM((rows, 2 * WIDE), jnp.bfloat16),
            pltpu.VMEM((steps, width, 2 * WIDE), jnp.bfloat16),
            pltpu.VMEM((steps, 3, 128, 2 * WIDE), jnp.bfloat16),
            pltpu.VMEM((steps, 64, 2 * WIDE), jnp.bfloat16),
            pltpu.VMEM((steps, 64, 2 * WIDE), jnp.float32),
            pltpu.VMEM((steps, 64, 2 * WIDE), jnp.bfloat16),
            pltpu.VMEM((CHUNKS, 8, WIDE), jnp.float32),
            pltpu.VMEM((3, CHUNKS, 8, WIDE), jnp.float32),
            pltpu.VMEM((2, CHUNKS, 2, 8, WIDE), jnp.float32),
            pltpu.VMEM((128, 128), jnp.int32),
            pltpu.VMEM((3, CHUNKS, 8, WIDE), jnp.float32),
            pltpu.VMEM((3, 128, 128), jnp.float32),
            dma((CHUNKS,)),
            dma((2, CHUNKS)), dma((2, CHUNKS)), dma((2, CHUNKS)), dma((2, CHUNKS)),
            dma((2,)), dma((2,)), dma((2,)), dma((2,)),
            dma((7,)), dma((7,)),
            dma((steps, 3)), dma((steps, 3)), dma((steps,)), dma((steps,)),
            pltpu.SemaphoreType.REGULAR,
        ],
        compiler_params=pltpu.CompilerParams(
            collective_id=0, has_side_effects=True, vmem_limit_bytes=60 * 2**20
        ),
    )(dosage, positions.reshape(-1, WIDE), partners)


def per_device(dosage, positions, partners):
    masked = tiles(dosage, positions, partners)
    share_rows = masked.shape[2]
    return masked.transpose(2, 0, 1, 3).reshape(share_rows, partners.shape[0], dosage.shape[1]).astype(jnp.bfloat16)


def solution(mesh):
    return jax.shard_map(
        per_device,
        mesh=mesh,
        in_specs=(P("ind", "var"), P(), P("var")),
        out_specs=P("ind", "var", None),
        check_vma=False,
    )
```
